128 devices in a mesh: dev: 128 (over y, z, x, core).
Axes of the slice: x: 4, y: 4, z: 4, core: 2. Of those that a mesh axis runs over, the one named last changes fastest.
Arguments:
- runs_field: float32 [2048, 256, 256], P('dev'), may hold values from -6 to 6
- spectral_filter: float32 [256, 129], replicated, may hold values from 0.3 to 3, as said below
- block_inverses: float32 [2, 256, 256], replicated, may hold values from -1.5 to 1.5, as said below
- factor_panels: float32 [2, 2048, 256], P(None, 'dev'), may hold values from -0.375 to 0.375
Outputs:
- solved: float32 [2048, 65536], P(None, 'dev')
The draws below stay inside these ranges and needn't reach their ends.
Inputs may be any that keep to these rules, and one draw needn't show every extreme that they name: `spectral_filter`: symmetric under the first frequency index k -> (256 - k) mod 256 in columns 0 and 128. `block_inverses`: each block is lower triangular with diagonal entries from 0.7 to 1.4.
All inputs are finite; a program needn't handle non-finite values.
Results may differ from the reference program's by a relative error of at most 0.000076.
Values sent between devices are 32-bit elements; how exact they have to be, the bound alone decides.
A program may use at most 64 MiB of HBM per device.

```python
import jax
import jax.numpy as jnp
from jax import lax

GRID = 256
PANEL = 256
RUNS = 2048
HALF = 129


def draw_spectral_filter(key, part):
    logs = jax.random.uniform(key, (GRID, HALF), jnp.float32, jnp.log(0.3), jnp.log(3.0))
    mirrored = jnp.roll(jnp.flip(logs, 0), 1, 0)
    column = jnp.arange(HALF, dtype=jnp.int32)[None, :]
    edges = (column == 0) | (column == HALF - 1)
    logs = jnp.where(edges, 0.5 * (logs + mirrored), logs)
    return jnp.exp(logs).astype(jnp.float32)


def draw_block_inverses(key, part):
    key_low, key_diag = jax.random.split(key)
    rows = jnp.arange(PANEL, dtype=jnp.int32)[:, None]
    cols = jnp.arange(PANEL, dtype=jnp.int32)[None, :]
    lower = (rows > cols).astype(jnp.float32)
    below = jax.random.truncated_normal(key_low, -3.0, 3.0, (2, PANEL, PANEL), jnp.float32)
    diagonal = jax.random.uniform(key_diag, (2, PANEL), jnp.float32, 0.7, 1.4)
    eye = (rows == cols).astype(jnp.float32)
    blocks = below * lower * (0.6 / PANEL ** 0.5) + diagonal[:, :, None] * eye
    return blocks.astype(jnp.float32)


def level_of(rng, extent, cuts, smallest, largest):
    factor_of = 1.0
    for dim, shards_of in cuts:
        steps = jax.random.uniform(jax.random.fold_in(jax.random.fold_in(rng, 6), dim), (shards_of,), jnp.float32, smallest / len(cuts), largest / len(cuts))
        factor_of = factor_of * jnp.repeat(jnp.exp(steps), extent[dim] // shards_of).reshape((-1,) + (1,) * (len(extent) - 1 - dim))
    return factor_of


def centred(own_key, extent, scale, limit, shards=(), kind=jnp.bfloat16):
    gain = level_of(own_key, extent, shards, -0.22, 0.18) if shards else 1.0
    result = jax.random.normal(own_key, extent, jnp.float32) * scale * gain
    return jnp.minimum(jnp.maximum(result, -limit), limit).astype(kind)


def setup_inputs(seed: int = 0) -> dict:
    streams_of = jax.random.split(jax.random.key(seed), 5)
    return {
        "runs_field": centred(streams_of[0], (RUNS, GRID, GRID), 1.0, 6.0, ((0, 128),), jnp.float32),
        "spectral_filter": draw_spectral_filter(jax.random.fold_in(streams_of[4], 71), 0),
        "block_inverses": draw_block_inverses(jax.random.fold_in(streams_of[4], 71), 0),
        "factor_panels": centred(streams_of[3], (2, RUNS, PANEL), PANEL ** -0.5, 0.375, ((1, 128),), jnp.float32),
    }


def reference(runs_field, spectral_filter, block_inverses, factor_panels):
    precise = lax.Precision.HIGHEST

    def whiten_one(one_run):
        spectrum = jnp.fft.rfft2(one_run) * spectral_filter
        return jnp.fft.irfft2(spectrum, s=(GRID, GRID)).astype(jnp.float32)

    whitened = lax.map(whiten_one, runs_field).reshape(RUNS, GRID * GRID)
    first = jnp.dot(block_inverses[0], whitened[:PANEL], precision=precise, preferred_element_type=jnp.float32)
    remain_one = whitened[PANEL:] - jnp.dot(factor_panels[0, PANEL:], first, precision=precise, preferred_element_type=jnp.float32)
    second = jnp.dot(block_inverses[1], remain_one[:PANEL], precision=precise, preferred_element_type=jnp.float32)
    remain_two = remain_one[PANEL:] - jnp.dot(factor_panels[1, 2 * PANEL:], second, precision=precise, preferred_element_type=jnp.float32)
    return jnp.concatenate([first, second, remain_two], axis=0)
```

```python
import math

import jax
import jax.numpy as jnp
from jax import lax
from jax.experimental import pallas as pl
from jax.experimental.pallas import tpu as pltpu
from jax.sharding import PartitionSpec as P

MESH = pl.DeviceIdType.MESH


def dft_tables(length):
    index = jnp.arange(length, dtype=jnp.int32)
    phase = index[:, None] * index[None, :] % length
    angle = phase.astype(jnp.float32) * (2.0 * math.pi / length)
    return (jnp.cos(angle), jnp.sin(angle))


def whiten(runs_field, spectral_filter):
    precise = lax.Precision.HIGH
    length = runs_field.shape[1]
    half_size = length // 2 + 1
    cosine_table, sine_table = dft_tables(length)
    cosine_half = cosine_table[:, :half_size]
    sine_half = sine_table[:, :half_size]
    real_cols = jnp.einsum("rmn,nk->rmk", runs_field, cosine_half, precision=precise)
    imag_cols = -jnp.einsum("rmn,nk->rmk", runs_field, sine_half, precision=precise)
    real_freq = jnp.einsum("am,rmk->rak", cosine_table, real_cols, precision=precise) + jnp.einsum(
        "am,rmk->rak", sine_table, imag_cols, precision=precise
    )
    imag_freq = jnp.einsum("am,rmk->rak", cosine_table, imag_cols, precision=precise) - jnp.einsum(
        "am,rmk->rak", sine_table, real_cols, precision=precise
    )
    real_freq = real_freq * spectral_filter
    imag_freq = imag_freq * spectral_filter
    real_back = jnp.einsum("am,rmk->rak", cosine_table, real_freq, precision=precise) - jnp.einsum(
        "am,rmk->rak", sine_table, imag_freq, precision=precise
    )
    imag_back = jnp.einsum("am,rmk->rak", cosine_table, imag_freq, precision=precise) + jnp.einsum(
        "am,rmk->rak", sine_table, real_freq, precision=precise
    )
    column = jnp.arange(half_size, dtype=jnp.int32)
    edges = (column == 0) | (column == length // 2)
    weights = jnp.where(edges, 1.0, 2.0).astype(jnp.float32) / float(length * length)
    real_back = real_back * weights
    imag_back = imag_back * weights
    result = jnp.einsum("rak,nk->ran", real_back, cosine_half, precision=precise) - jnp.einsum(
        "rak,nk->ran", imag_back, sine_half, precision=precise
    )
    return result


def exchange_kernel(x_ref, o_ref, ssem, rsem, lsem):
    me = lax.axis_index("dev")
    bar = pltpu.get_barrier_semaphore()

    def greet(k, carry):
        pl.semaphore_signal(bar, inc=1, device_id=(lax.rem(me + k, 128),), device_id_type=MESH)
        return carry

    lax.fori_loop(1, 128, greet, 0)
    pl.semaphore_wait(bar, 127)
    mine = pl.ds(pl.multiple_of(me * 16, 16), 16)
    y, z, x, c = me // 32, (me // 8) % 4, (me // 2) % 4, me % 2

    def send(k, carry):
        dx = k % 4
        dy = (dx + (k // 4) % 4) % 4
        dz = (dx + (k // 16) % 4) % 4
        d = ((((y + dy) % 4) * 4 + (z + dz) % 4) * 4 + (x + dx) % 4) * 2 + (c + k // 64) % 2
        src = x_ref.at[pl.ds(pl.multiple_of(d * 16, 16), 16)]
        pltpu.make_async_remote_copy(
            src, o_ref.at[mine], ssem, rsem, device_id=(d,), device_id_type=MESH
        ).start()
        return carry

    lax.fori_loop(1, 128, send, 0)
    local = pltpu.make_async_copy(x_ref.at[mine], o_ref.at[mine], lsem)
    local.start()
    local.wait()
    rest = pl.ds(0, 127 * 16)
    whole = pltpu.make_async_remote_copy(
        x_ref.at[rest], o_ref.at[rest], ssem, rsem,
        device_id=(lax.rem(me + 1, 128),), device_id_type=MESH,
    )
    whole.wait_send()
    whole.wait_recv()


def exchange(x):
    return pl.pallas_call(
        exchange_kernel,
        out_shape=jax.ShapeDtypeStruct((2048, 512), jnp.float32),
        in_specs=[pl.BlockSpec(memory_space=pl.ANY)],
        out_specs=pl.BlockSpec(memory_space=pl.ANY),
        scratch_shapes=[pltpu.SemaphoreType.DMA] * 3,
        compiler_params=pltpu.CompilerParams(collective_id=0, has_side_effects=True),
    )(x)


def per_device(runs_field, spectral_filter, block_inverses, factor_panels):
    high = lax.Precision.HIGH
    whitened = whiten(runs_field, spectral_filter).reshape(16, 128, 512)
    panels = lax.all_gather(factor_panels, "dev", axis=1, tiled=True)
    cells = exchange(whitened.transpose(1, 0, 2).reshape(2048, 512))
    first = jnp.dot(block_inverses[0], cells[:256], precision=high)
    rest = cells[256:] - jnp.dot(panels[0, 256:], first, precision=high)
    second = jnp.dot(block_inverses[1], rest[:256], precision=high)
    last = rest[256:] - jnp.dot(panels[1, 512:], second, precision=high)
    return jnp.concatenate([first, second, last], axis=0)


def solution(mesh):
    return jax.shard_map(
        per_device,
        mesh=mesh,
        in_specs=(P("dev", None, None), P(), P(), P(None, "dev", None)),
        out_specs=P(None, "dev"),
        check_vma=False,
    )
```

```python
import math

import jax
import jax.numpy as jnp
import numpy as np
from jax import lax
from jax.experimental import pallas as pl
from jax.experimental.pallas import tpu as pltpu
from jax.sharding import PartitionSpec as P

MESH = pl.DeviceIdType.MESH
F32, BF16 = jnp.float32, jnp.bfloat16
N, HALF = 256, 128
DEVS = 128
GROUP = 4


def tables():
    n = np.arange(N)[:, None]
    k = np.arange(HALF)[None, :]
    angle = 2.0 * math.pi * ((n * k) % N) / N
    low = np.sin(angle)
    low[:, 0] = np.where(np.arange(N) % 2 == 0, 1.0, -1.0)
    v = np.concatenate([np.cos(angle), low], axis=1).astype(np.float32)
    high = v.astype(jnp.bfloat16)
    rest = (v - high.astype(np.float32)).astype(jnp.bfloat16)
    return np.stack([high, rest, high.T, rest.T])


def split(value):
    high = value.astype(BF16)
    return high, (value - high.astype(F32)).astype(BF16)


def dot(a, b):
    return jnp.dot(a, b, preferred_element_type=F32)


def dot3(a, b):
    return dot(a[0], b[0]) + (dot(a[0], b[1]) + dot(a[1], b[0]))


def coefficients(filter_t):
    row = lax.broadcasted_iota(jnp.int32, (HALF, N), 0)
    col = lax.broadcasted_iota(jnp.int32, (HALF, N), 1)
    same = (row == col).astype(F32)
    other = ((row + col == N) & (row > 0)).astype(F32)
    nyquist = ((row == 0) & (col == HALF)).astype(F32)
    not_zero = (row > 0).astype(F32)
    picks = [same + other, (same + other) * not_zero + nyquist, (same - other) * not_zero]
    pick = jnp.concatenate(picks, axis=0).astype(BF16)
    one = filter_t.astype(BF16)
    left = filter_t - one.astype(F32)
    two = left.astype(BF16)
    three = (left - two.astype(F32)).astype(BF16)

    def take(part):
        return lax.dot_general(pick, part, (((1,), (1,)), ((), ())), preferred_element_type=F32)

    mixed = (take(three) + take(two)) + take(one)
    lane = lax.broadcasted_iota(jnp.int32, (3 * HALF, HALF), 1)
    scale = jnp.where(lane == 0, 1.0, 2.0).astype(F32) / float(N * N)
    p = mixed[:, :HALF]
    q = jnp.where(lane == 0, mixed[:, HALF : HALF + 1], p)
    p, q = p * scale, q * scale
    even = jnp.concatenate([p[: 2 * HALF], q[: 2 * HALF]], axis=1)
    odd_p, odd_q = p[2 * HALF :], q[2 * HALF :]
    odd = jnp.concatenate(
        [jnp.concatenate([-odd_q, odd_p], axis=1), jnp.concatenate([odd_q, -odd_p], axis=1)], axis=0
    )
    return even, odd


def front_kernel(
    x_hbm, filt_hbm, inv_hbm, pan_hbm, tab_hbm, land, gh_hbm, gl_hbm,
    x, filt, inv, tab, even, odd, out, gath, pan, gh, gl,
    xsem, csem, psem, gsem, a_send, a_recv, g_send, g_recv, lsem,
):
    me = lax.axis_index("dev")
    y, z, xx, c = me // 32, (me // 8) % 4, (me // 2) % 4, me % 2
    partner = me + 1 - 2 * c
    bar = pltpu.get_barrier_semaphore()

    def greet(k, carry):
        pl.semaphore_signal(bar, inc=1, device_id=(lax.rem(me + k, DEVS),), device_id_type=MESH)
        return carry

    def place(u, core, cx, cz, cy):
        rot = (core * 4 + u) % 3
        first = jnp.where(rot == 0, cx, jnp.where(rot == 1, cz, cy))
        middle = jnp.where(rot == 0, cz, jnp.where(rot == 1, cy, cx))
        last = jnp.where(rot == 0, cy, jnp.where(rot == 1, cx, cz))
        return last, middle, first

    def own(u):
        last, middle, first = place(u, c, xx, z, y)
        return gath.at[u, c, last, middle, first]

    consts = [
        pltpu.make_async_copy(filt_hbm, filt, csem.at[0]),
        pltpu.make_async_copy(tab_hbm, tab, csem.at[1]),
        pltpu.make_async_copy(inv_hbm, inv, csem.at[2]),
    ]
    units = [
        pltpu.make_async_copy(pan_hbm.at[u // 2, pl.ds(8 * (u % 2), 8)], own(u), psem.at[u])
        for u in range(4)
    ]
    runs = [pltpu.make_async_copy(x_hbm.at[pl.ds(GROUP * i, GROUP)], x.at[pl.ds(GROUP * i, GROUP)], xsem.at[i])
            for i in range(4)]
    for copy in consts[:2] + units + runs + consts[2:]:
        copy.start()
    lax.fori_loop(1, DEVS, greet, 0)

    consts[0].wait()
    consts[1].wait()
    e, o = coefficients(filt[...])
    even[...] = e
    odd[...] = o

    for copy in units:
        copy.wait()
    pl.semaphore_wait(bar, DEVS - 1)

    def gather_start(phase):
        for u in range(4):
            last, middle, first = place(u, c, xx, z, y)
            axis = ((c * 4 + u) % 3 + phase) % 3
            stride = jnp.where(axis == 0, 2, jnp.where(axis == 1, 8, 32))
            at = jnp.where(axis == 0, xx, jnp.where(axis == 1, z, y))
            block = [gath.at[u, c, last, middle, first], gath.at[u, c, last, middle], gath.at[u, c, last]][phase]
            for step in (1, 3, 2):
                to = me + ((at + step) % 4 - at) * stride
                pltpu.make_async_remote_copy(
                    block, block, g_send.at[u, phase], g_recv.at[u, phase],
                    device_id=(to,), device_id_type=MESH,
                ).start()

    def gather_wait(phase):
        for u in range(4):
            three = pl.ds(0, 3)
            block = [gath.at[u, c, 0, 0, three], gath.at[u, c, 0, three], gath.at[u, c, three]][phase]
            whole = pltpu.make_async_remote_copy(
                block, block, g_send.at[u, phase], g_recv.at[u, phase],
                device_id=(partner,), device_id_type=MESH,
            )
            whole.wait_send()
            whole.wait_recv()

    def whiten(i):
        runs[i].wait()
        v, vt = (tab[0], tab[1]), (tab[2], tab[3])
        half = i // 2
        base = GROUP * (i % 2)
        rows = x[GROUP * i : GROUP * (i + 1)].reshape(GROUP * N, N)
        cols = dot3(split(rows), v)
        backs = []
        for g in range(GROUP):
            t = dot3(vt, split(cols[g * N : (g + 1) * N]))
            low, up = t[:HALF], t[HALF:]
            turned = jnp.concatenate(
                [
                    jnp.concatenate([up[:, HALF:], up[:, :HALF]], axis=1),
                    jnp.concatenate([low[:, HALF:], low[:, :HALF]], axis=1),
                ],
                axis=0,
            )
            backs.append(even[...] * t + odd[...] * turned)
        spread = dot3(split(jnp.concatenate(backs, axis=0)), vt)
        for g in range(GROUP):
            done = dot3(v, split(spread[g * N : (g + 1) * N]))
            for h in range(2):
                out[half, h, pl.ds(base + g, N, stride=8), :] = done[:, h * HALF : (h + 1) * HALF]

    def send_half(half):
        def send(k, carry):
            dx = k % 4
            dy = (dx + (k // 4) % 4) % 4
            dz = (dx + (k // 16) % 4) % 4
            d = ((((y + dy) % 4) * 4 + (z + dz) % 4) * 4 + (xx + dx) % 4) * 2 + (c + k // 64) % 2
            pltpu.make_async_remote_copy(
                out.at[half, :, pl.ds(pl.multiple_of(d * 16, 16), 16)], land.at[:, me, half],
                a_send.at[half], a_recv.at[half], device_id=(d,), device_id_type=MESH,
            ).start()
            return carry

        lax.fori_loop(1, DEVS, send, 0)
        return pltpu.make_async_copy(
            out.at[half, :, pl.ds(pl.multiple_of(me * 16, 16), 16)], land.at[:, me, half], lsem.at[half]
        )

    gather_start(0)
    whiten(0)
    gather_wait(0)
    gather_start(1)
    whiten(1)
    gather_wait(1)
    gather_start(2)
    local0 = send_half(0)
    local0.start()
    whiten(2)
    whiten(3)
    local1 = send_half(1)
    local1.start()
    gather_wait(2)

    swaps = []
    for u in range(4):
        block = gath.at[u, c]
        swap = pltpu.make_async_remote_copy(
            block, block, g_send.at[u, 3], g_recv.at[u, 3], device_id=(partner,), device_id_type=MESH
        )
        swap.start()
        swaps.append(swap)
    for swap in swaps:
        swap.wait_send()
        swap.wait_recv()
    consts[2].wait()

    def order(d, carry):
        cy, cz, cx, core = d // 32, (d // 8) % 4, (d // 2) % 4, d % 2
        for u in range(4):
            last, middle, first = place(u, core, cx, cz, cy)
            to = pl.ds(pl.multiple_of(d * 16 + 8 * (u % 2), 8), 8)
            pan[u // 2, to, :] = gath[u, core, last, middle, first]
        return carry

    lax.fori_loop(0, DEVS, order, 0)

    b0, b1 = split(inv[0]), split(inv[1])
    joined = dot3(split(pan[0, N : 2 * N, :]), b0)
    joined_parts = split(joined)
    cross = dot3(b1, joined_parts)

    def put(start, left, right):
        lh, ll = split(left)
        rh, rl = split(right)
        rows = pl.ds(start, N)
        gh[rows, :N] = lh
        gl[rows, :N] = ll
        gh[rows, N:] = rh
        gl[rows, N:] = rl

    put(0, inv[0], jnp.zeros((N, N), F32))
    put(N, -cross, inv[1])

    def combine(i, carry):
        start = pl.multiple_of(i * N, N)
        h1 = dot3(split(pan[1, pl.ds(start, N), :]), b1)
        h0 = dot3(split(pan[0, pl.ds(start, N), :]), b0) - dot3(split(h1), joined_parts)
        put(start, -h0, -h1)
        return carry

    lax.fori_loop(2, 8, combine, 0)
    outs = [
        pltpu.make_async_copy(gh, gh_hbm, gsem.at[0]),
        pltpu.make_async_copy(gl, gl_hbm, gsem.at[1]),
    ]
    for copy in outs:
        copy.start()
    for copy in outs:
        copy.wait()
    local0.wait()
    local1.wait()
    for half in range(2):
        rest = pl.ds(0, (DEVS - 1) * 16)
        whole = pltpu.make_async_remote_copy(
            out.at[half, :, rest], out.at[half, :, rest], a_send.at[half], a_recv.at[half],
            device_id=(partner,), device_id_type=MESH,
        )
        whole.wait_send()
        whole.wait_recv()


def front(runs_field, filter_t, block_inverses, factor_panels, table):
    anywhere = pl.BlockSpec(memory_space=pl.ANY)
    return pl.pallas_call(
        front_kernel,
        out_shape=(
            jax.ShapeDtypeStruct((2, DEVS, 2, 16, HALF), F32),
            jax.ShapeDtypeStruct((2048, 512), BF16),
            jax.ShapeDtypeStruct((2048, 512), BF16),
        ),
        in_specs=[anywhere] * 5,
        out_specs=(anywhere,) * 3,
        scratch_shapes=[
            pltpu.VMEM((16, N, N), F32),
            pltpu.VMEM((129, N), F32),
            pltpu.VMEM((2, N, N), F32),
            pltpu.VMEM((4, N, N), BF16),
            pltpu.VMEM((N, N), F32),
            pltpu.VMEM((N, N), F32),
            pltpu.VMEM((2, 2, 2048, HALF), F32),
            pltpu.VMEM((4, 2, 4, 4, 4, 8, N), F32),
            pltpu.VMEM((2, 2048, N), F32),
            pltpu.VMEM((2048, 512), BF16),
            pltpu.VMEM((2048, 512), BF16),
            pltpu.SemaphoreType.DMA((4,)),
            pltpu.SemaphoreType.DMA((3,)),
            pltpu.SemaphoreType.DMA((4,)),
            pltpu.SemaphoreType.DMA((2,)),
            pltpu.SemaphoreType.DMA((2,)),
            pltpu.SemaphoreType.DMA((2,)),
            pltpu.SemaphoreType.DMA((4, 4)),
            pltpu.SemaphoreType.DMA((4, 4)),
            pltpu.SemaphoreType.DMA((2,)),
        ],
        compiler_params=pltpu.CompilerParams(
            collective_id=0, has_side_effects=True, vmem_limit_bytes=56 << 20
        ),
        name="front",
    )(runs_field, filter_t, block_inverses, factor_panels, table)


def unpack(block):
    sources = block.shape[1]
    parts = []
    for row in range(2):
        for h in range(2):
            part = block[h, :, :, 8 * row : 8 * row + 8, :]
            parts.append(part.reshape(sources * 16, HALF))
    return jnp.concatenate(parts, axis=1)


def solve_kernel(top_ref, w_ref, gh_ref, gl_ref, o_ref, wh, wl):
    step = pl.program_id(0)

    @pl.when(step == 0)
    def _():
        high, low = split(unpack(top_ref))
        wh[...] = high
        wl[...] = low

    product = dot3((gh_ref[...], gl_ref[...]), (wh[...], wl[...]))
    rows = o_ref.shape[0]
    solved = step * rows < 512

    @pl.when(solved)
    def _():
        o_ref[...] = product

    @pl.when(jnp.logical_not(solved))
    def _():
        o_ref[...] = product + unpack(w_ref)


def solve(landed, gh, gl):
    rows = 256
    return pl.pallas_call(
        solve_kernel,
        grid=(2048 // rows,),
        out_shape=jax.ShapeDtypeStruct((2048, 512), F32),
        in_specs=[
            pl.BlockSpec((2, 32, 2, 16, HALF), lambda i: (0, 0, 0, 0, 0)),
            pl.BlockSpec((2, rows // 16, 2, 16, HALF), lambda i: (0, i, 0, 0, 0)),
            pl.BlockSpec((rows, 512), lambda i: (i, 0)),
            pl.BlockSpec((rows, 512), lambda i: (i, 0)),
        ],
        out_specs=pl.BlockSpec((rows, 512), lambda i: (i, 0)),
        scratch_shapes=[pltpu.VMEM((512, 512), BF16), pltpu.VMEM((512, 512), BF16)],
        compiler_params=pltpu.CompilerParams(vmem_limit_bytes=40 << 20),
        name="solve",
    )(landed, landed, gh, gl)


def per_device(runs_field, spectral_filter, block_inverses, factor_panels):
    landed, gh, gl = front(
        runs_field, spectral_filter.T, block_inverses, factor_panels, jnp.asarray(tables())
    )
    return solve(landed, gh, gl)


def solution(mesh):
    return jax.shard_map(
        per_device,
        mesh=mesh,
        in_specs=(P("dev", None, None), P(), P(), P(None, "dev", None)),
        out_specs=P(None, "dev"),
        check_vma=False,
    )
```

```python
import math

import jax
import jax.numpy as jnp
import numpy as np
from jax import lax
from jax.experimental import pallas as pl
from jax.experimental.pallas import tpu as pltpu
from jax.sharding import PartitionSpec as P

MESH = pl.DeviceIdType.MESH
F32, BF16 = jnp.float32, jnp.bfloat16
N, HALF = 256, 128
DEVS = 128
GROUP = 4


def tables():
    n = np.arange(N)[:, None]
    k = np.arange(HALF)[None, :]
    angle = 2.0 * math.pi * ((n * k) % N) / N
    low = np.sin(angle)
    low[:, 0] = np.where(np.arange(N) % 2 == 0, 1.0, -1.0)
    v = np.concatenate([np.cos(angle), low], axis=1).astype(np.float32)
    high = v.astype(jnp.bfloat16)
    rest = (v - high.astype(np.float32)).astype(jnp.bfloat16)
    return np.stack([high, rest, high.T, rest.T])


def split(value):
    high = value.astype(BF16)
    return high, (value - high.astype(F32)).astype(BF16)


def dot(a, b):
    return jnp.dot(a, b, preferred_element_type=F32)


def dot3(a, b):
    return dot(a[0], b[0]) + (dot(a[0], b[1]) + dot(a[1], b[0]))


def coefficients(filter_t):
    row = lax.broadcasted_iota(jnp.int32, (HALF, N), 0)
    col = lax.broadcasted_iota(jnp.int32, (HALF, N), 1)
    same = (row == col).astype(F32)
    other = ((row + col == N) & (row > 0)).astype(F32)
    nyquist = ((row == 0) & (col == HALF)).astype(F32)
    not_zero = (row > 0).astype(F32)
    picks = [same + other, (same + other) * not_zero + nyquist, (same - other) * not_zero]
    pick = jnp.concatenate(picks, axis=0).astype(BF16)
    one = filter_t.astype(BF16)
    left = filter_t - one.astype(F32)
    two = left.astype(BF16)
    three = (left - two.astype(F32)).astype(BF16)

    def take(part):
        return lax.dot_general(pick, part, (((1,), (1,)), ((), ())), preferred_element_type=F32)

    mixed = (take(three) + take(two)) + take(one)
    lane = lax.broadcasted_iota(jnp.int32, (3 * HALF, HALF), 1)
    scale = jnp.where(lane == 0, 1.0, 2.0).astype(F32) / float(N * N)
    p = mixed[:, :HALF]
    q = jnp.where(lane == 0, mixed[:, HALF : HALF + 1], p)
    p, q = p * scale, q * scale
    even = jnp.concatenate([p[: 2 * HALF], q[: 2 * HALF]], axis=1)
    odd_p, odd_q = p[2 * HALF :], q[2 * HALF :]
    odd = jnp.concatenate(
        [jnp.concatenate([-odd_q, odd_p], axis=1), jnp.concatenate([odd_q, -odd_p], axis=1)], axis=0
    )
    return even, odd


def front_kernel(
    x_hbm, filt_hbm, inv_hbm, pan_hbm, tab_hbm, o_hbm,
    x, filt, inv, tab, even, odd, out, land, gath, pan, factor, acc, wh, wl,
    xsem, csem, psem, osem, a_send, a_recv, g_send, g_recv, lsem,
):
    me = lax.axis_index("dev")
    y, z, xx, c = me // 32, (me // 8) % 4, (me // 2) % 4, me % 2
    partner = me + 1 - 2 * c
    bar = pltpu.get_barrier_semaphore()

    def greet(k, carry):
        pl.semaphore_signal(bar, inc=1, device_id=(lax.rem(me + k, DEVS),), device_id_type=MESH)
        return carry

    def place(u, core, cx, cz, cy):
        rot = (core * 4 + u) % 3
        first = jnp.where(rot == 0, cx, jnp.where(rot == 1, cz, cy))
        middle = jnp.where(rot == 0, cz, jnp.where(rot == 1, cy, cx))
        last = jnp.where(rot == 0, cy, jnp.where(rot == 1, cx, cz))
        return last, middle, first

    def own(u):
        last, middle, first = place(u, c, xx, z, y)
        return gath.at[u, c, last, middle, first]

    consts = [
        pltpu.make_async_copy(filt_hbm, filt, csem.at[0]),
        pltpu.make_async_copy(tab_hbm, tab, csem.at[1]),
        pltpu.make_async_copy(inv_hbm, inv, csem.at[2]),
    ]
    units = [
        pltpu.make_async_copy(pan_hbm.at[u // 2, pl.ds(8 * (u % 2), 8)], own(u), psem.at[u])
        for u in range(4)
    ]
    runs = [pltpu.make_async_copy(x_hbm.at[pl.ds(GROUP * i, GROUP)], x.at[pl.ds(GROUP * i, GROUP)], xsem.at[i])
            for i in range(4)]
    for copy in consts[:2] + units + runs + consts[2:]:
        copy.start()
    lax.fori_loop(1, DEVS, greet, 0)

    for copy in units:
        copy.wait()
    pl.semaphore_wait(bar, DEVS - 1)

    def gather_start(phase):
        for u in range(4):
            last, middle, first = place(u, c, xx, z, y)
            axis = ((c * 4 + u) % 3 + phase) % 3
            stride = jnp.where(axis == 0, 2, jnp.where(axis == 1, 8, 32))
            at = jnp.where(axis == 0, xx, jnp.where(axis == 1, z, y))
            block = [gath.at[u, c, last, middle, first], gath.at[u, c, last, middle], gath.at[u, c, last]][phase]
            for step in (1, 3, 2):
                to = me + ((at + step) % 4 - at) * stride
                pltpu.make_async_remote_copy(
                    block, block, g_send.at[u, phase], g_recv.at[u, phase],
                    device_id=(to,), device_id_type=MESH,
                ).start()

    def gather_wait(phase):
        for u in range(4):
            three = pl.ds(0, 3)
            block = [gath.at[u, c, 0, 0, three], gath.at[u, c, 0, three], gath.at[u, c, three]][phase]
            whole = pltpu.make_async_remote_copy(
                block, block, g_send.at[u, phase], g_recv.at[u, phase],
                device_id=(partner,), device_id_type=MESH,
            )
            whole.wait_send()
            whole.wait_recv()

    def whiten(i):
        runs[i].wait()
        v, vt = (tab[0], tab[1]), (tab[2], tab[3])
        rows = x[GROUP * i : GROUP * (i + 1)].reshape(GROUP * N, N)
        cols = dot3(split(rows), v)
        backs = []
        for g in range(GROUP):
            t = dot3(vt, split(cols[g * N : (g + 1) * N]))
            low, up = t[:HALF], t[HALF:]
            turned = jnp.concatenate(
                [
                    jnp.concatenate([up[:, HALF:], up[:, :HALF]], axis=1),
                    jnp.concatenate([low[:, HALF:], low[:, :HALF]], axis=1),
                ],
                axis=0,
            )
            backs.append(even[...] * t + odd[...] * turned)
        spread = dot3(split(jnp.concatenate(backs, axis=0)), vt)
        for g in range(GROUP):
            done = dot3(v, split(spread[g * N : (g + 1) * N]))
            for h in range(2):
                out[i, h, pl.ds(g, N, stride=GROUP), :] = done[:, h * HALF : (h + 1) * HALF]

    def send_part(part):
        def send(k, carry):
            dx = k % 4
            dy = (dx + (k // 4) % 4) % 4
            dz = (dx + (k // 16) % 4) % 4
            d = ((((y + dy) % 4) * 4 + (z + dz) % 4) * 4 + (xx + dx) % 4) * 2 + (c + k // 64) % 2
            pltpu.make_async_remote_copy(
                out.at[part, :, pl.ds(pl.multiple_of(d * 8, 8), 8)], land.at[:, part, me],
                a_send.at[part], a_recv.at[part], device_id=(d,), device_id_type=MESH,
            ).start()
            return carry

        lax.fori_loop(1, DEVS, send, 0)
        local = pltpu.make_async_copy(
            out.at[part, :, pl.ds(pl.multiple_of(me * 8, 8), 8)], land.at[:, part, me], lsem.at[part]
        )
        local.start()
        return local

    def arrived(part):
        locals_[part].wait()
        rest = pl.ds(0, (DEVS - 1) * 8)
        whole = pltpu.make_async_remote_copy(
            out.at[part, :, rest], out.at[part, :, rest], a_send.at[part], a_recv.at[part],
            device_id=(partner,), device_id_type=MESH,
        )
        whole.wait_send()
        whole.wait_recv()

    gather_start(0)
    consts[0].wait()
    consts[1].wait()
    e, o = coefficients(filt[...])
    even[...] = e
    odd[...] = o
    whiten(0)
    gather_wait(0)
    gather_start(1)
    locals_ = [send_part(0)]
    whiten(1)
    gather_wait(1)
    gather_start(2)
    locals_.append(send_part(1))
    for part in (2, 3):
        whiten(part)
        locals_.append(send_part(part))
    gather_wait(2)

    swaps = []
    for u in range(4):
        block = gath.at[u, c]
        swap = pltpu.make_async_remote_copy(
            block, block, g_send.at[u, 3], g_recv.at[u, 3], device_id=(partner,), device_id_type=MESH
        )
        swap.start()
        swaps.append(swap)
    for swap in swaps:
        swap.wait_send()
        swap.wait_recv()
    consts[2].wait()

    def order(d, carry):
        cy, cz, cx, core = d // 32, (d // 8) % 4, (d // 2) % 4, d % 2
        for u in range(4):
            last, middle, first = place(u, core, cx, cz, cy)
            to = pl.ds(pl.multiple_of(d * 16 + 8 * (u % 2), 8), 8)
            pan[u // 2, to, :] = gath[u, core, last, middle, first]
        return carry

    lax.fori_loop(0, DEVS, order, 0)

    b0, b1 = split(inv[0]), split(inv[1])
    joined = dot3(split(pan[0, N : 2 * N, :]), b0)
    joined_parts = split(joined)
    cross = dot3(b1, joined_parts)

    row = lax.broadcasted_iota(jnp.int32, (N, N), 0)
    col = lax.broadcasted_iota(jnp.int32, (N, N), 1)
    shuffle = (col == (row // 8 % 2) * HALF + row // 16 * 8 + row % 8).astype(BF16)

    def put(start, left, right):
        rows = pl.ds(start, N)
        for side, value in enumerate((left, right)):
            for level, part in enumerate(split(value)):
                moved = dot(part, shuffle).astype(BF16)
                for half in range(2):
                    factor[half, level, rows, HALF * side : HALF * (side + 1)] = moved[
                        :, HALF * half : HALF * (half + 1)
                    ]

    put(0, inv[0], jnp.zeros((N, N), F32))
    put(N, -cross, inv[1])

    def combine(i, carry):
        start = pl.multiple_of(i * N, N)
        h1 = dot3(split(pan[1, pl.ds(start, N), :]), b1)
        h0 = dot3(split(pan[0, pl.ds(start, N), :]), b0) - dot3(split(h1), joined_parts)
        put(start, -h0, -h1)
        return carry

    lax.fori_loop(2, 8, combine, 0)

    def rows_of(half, start, sources):
        lower = lax.broadcasted_iota(jnp.int32, (sources, 8, HALF), 1) < GROUP
        columns = [None] * 4
        for h in range(2):
            a = land[h, 2 * half, pl.ds(start, sources)]
            b = land[h, 2 * half + 1, pl.ds(start, sources)]
            columns[h] = jnp.where(lower, a, pltpu.roll(b, GROUP, 1))
            columns[2 + h] = jnp.where(lower, pltpu.roll(a, GROUP, 1), b)
        return jnp.concatenate(columns, axis=2)

    def multiply(half):
        high, low = split(rows_of(half, 0, 32).reshape(N, 512))
        wh[...] = high
        wl[...] = low

        def chunk(i, own):
            rows = pl.ds(pl.multiple_of(i * N, N), N)
            product = dot3((factor[half, 0, rows, :], factor[half, 1, rows, :]), (wh[...], wl[...]))
            if own:
                mine = rows_of(half, i * 16, 16)
                none = jnp.zeros_like(mine)
                both = [mine, none] if half == 0 else [none, mine]
                product = product + jnp.stack(both, axis=1).reshape(N, 512)
            if half == 0:
                acc[rows, :] = product
            else:
                acc[rows, :] = acc[rows, :] + product
                pltpu.make_async_copy(acc.at[rows], o_hbm.at[rows], osem.at[i]).start()

        for i in range(2):
            chunk(i, False)

        def later(i, carry):
            chunk(i, True)
            return carry

        lax.fori_loop(2, 8, later, 0)

    arrived(0)
    arrived(1)
    multiply(0)
    arrived(2)
    arrived(3)
    multiply(1)
    for i in range(8):
        rows = pl.ds(i * N, N)
        pltpu.make_async_copy(acc.at[rows], o_hbm.at[rows], osem.at[i]).wait()


def front(runs_field, filter_t, block_inverses, factor_panels, table):
    anywhere = pl.BlockSpec(memory_space=pl.ANY)
    return pl.pallas_call(
        front_kernel,
        out_shape=jax.ShapeDtypeStruct((2048, 512), F32),
        in_specs=[anywhere] * 5,
        out_specs=anywhere,
        scratch_shapes=[
            pltpu.VMEM((16, N, N), F32),
            pltpu.VMEM((129, N), F32),
            pltpu.VMEM((2, N, N), F32),
            pltpu.VMEM((4, N, N), BF16),
            pltpu.VMEM((N, N), F32),
            pltpu.VMEM((N, N), F32),
            pltpu.VMEM((4, 2, 1024, HALF), F32),
            pltpu.VMEM((2, 4, DEVS, 8, HALF), F32),
            pltpu.VMEM((4, 2, 4, 4, 4, 8, N), F32),
            pltpu.VMEM((2, 2048, N), F32),
            pltpu.VMEM((2, 2, 2048, N), BF16),
            pltpu.VMEM((2048, 512), F32),
            pltpu.VMEM((N, 512), BF16),
            pltpu.VMEM((N, 512), BF16),
            pltpu.SemaphoreType.DMA((4,)),
            pltpu.SemaphoreType.DMA((3,)),
            pltpu.SemaphoreType.DMA((4,)),
            pltpu.SemaphoreType.DMA((8,)),
            pltpu.SemaphoreType.DMA((4,)),
            pltpu.SemaphoreType.DMA((4,)),
            pltpu.SemaphoreType.DMA((4, 4)),
            pltpu.SemaphoreType.DMA((4, 4)),
            pltpu.SemaphoreType.DMA((4,)),
        ],
        compiler_params=pltpu.CompilerParams(
            collective_id=0, has_side_effects=True, vmem_limit_bytes=56 << 20
        ),
        name="front",
    )(runs_field, filter_t, block_inverses, factor_panels, table)


def per_device(runs_field, spectral_filter, block_inverses, factor_panels):
    return front(runs_field, spectral_filter.T, block_inverses, factor_panels, jnp.asarray(tables()))


def solution(mesh):
    return jax.shard_map(
        per_device,
        mesh=mesh,
        in_specs=(P("dev", None, None), P(), P(), P(None, "dev", None)),
        out_specs=P(None, "dev"),
        check_vma=False,
    )
```

```python
import math

import jax
import jax.numpy as jnp
import numpy as np
from jax import lax
from jax.experimental import pallas as pl
from jax.experimental.pallas import tpu as pltpu
from jax.sharding import PartitionSpec as P

MESH = pl.DeviceIdType.MESH
F32, BF16 = jnp.float32, jnp.bfloat16
N, HALF = 256, 128
DEVS = 128
GROUP = 4


def tables():
    n = np.arange(N)[:, None]
    k = np.arange(HALF)[None, :]
    angle = 2.0 * math.pi * ((n * k) % N) / N
    low = np.sin(angle)
    low[:, 0] = np.where(np.arange(N) % 2 == 0, 1.0, -1.0)
    v = np.concatenate([np.cos(angle), low], axis=1).astype(np.float32)
    high = v.astype(jnp.bfloat16)
    rest = (v - high.astype(np.float32)).astype(jnp.bfloat16)
    return np.stack([high, rest, high.T, rest.T])


def split(value):
    high = value.astype(BF16)
    return high, (value - high.astype(F32)).astype(BF16)


def dot(a, b):
    return jnp.dot(a, b, preferred_element_type=F32)


def dot3(a, b):
    return dot(a[0], b[0]) + (dot(a[0], b[1]) + dot(a[1], b[0]))


def coefficients(filter_t):
    row = lax.broadcasted_iota(jnp.int32, (HALF, N), 0)
    col = lax.broadcasted_iota(jnp.int32, (HALF, N), 1)
    same = (row == col).astype(F32)
    other = ((row + col == N) & (row > 0)).astype(F32)
    nyquist = ((row == 0) & (col == HALF)).astype(F32)
    not_zero = (row > 0).astype(F32)
    picks = [same + other, (same + other) * not_zero + nyquist, (same - other) * not_zero]
    pick = jnp.concatenate(picks, axis=0).astype(BF16)
    one = filter_t.astype(BF16)
    left = filter_t - one.astype(F32)
    two = left.astype(BF16)
    three = (left - two.astype(F32)).astype(BF16)

    def take(part):
        return lax.dot_general(pick, part, (((1,), (1,)), ((), ())), preferred_element_type=F32)

    mixed = (take(three) + take(two)) + take(one)
    lane = lax.broadcasted_iota(jnp.int32, (3 * HALF, HALF), 1)
    scale = jnp.where(lane == 0, 1.0, 2.0).astype(F32) / float(N * N)
    p = mixed[:, :HALF]
    q = jnp.where(lane == 0, mixed[:, HALF : HALF + 1], p)
    p, q = p * scale, q * scale
    even = jnp.concatenate([p[: 2 * HALF], q[: 2 * HALF]], axis=1)
    odd_p, odd_q = p[2 * HALF :], q[2 * HALF :]
    odd = jnp.concatenate(
        [jnp.concatenate([-odd_q, odd_p], axis=1), jnp.concatenate([odd_q, -odd_p], axis=1)], axis=0
    )
    return even, odd


def front_kernel(
    x_hbm, filt_hbm, inv_hbm, pan_hbm, tab_hbm, acc,
    x, filt, inv, tab, even, odd, out, land, gath, pan, factor, wh, wl,
    xsem, csem, psem, a_send, a_recv, g_send, g_recv, lsem,
):
    me = lax.axis_index("dev")
    y, z, xx, c = me // 32, (me // 8) % 4, (me // 2) % 4, me % 2
    partner = me + 1 - 2 * c
    bar = pltpu.get_barrier_semaphore()

    def greet(k, carry):
        pl.semaphore_signal(bar, inc=1, device_id=(lax.rem(me + k, DEVS),), device_id_type=MESH)
        return carry

    def place(u, core, cx, cz, cy):
        rot = (core * 4 + u) % 3
        first = jnp.where(rot == 0, cx, jnp.where(rot == 1, cz, cy))
        middle = jnp.where(rot == 0, cz, jnp.where(rot == 1, cy, cx))
        last = jnp.where(rot == 0, cy, jnp.where(rot == 1, cx, cz))
        return last, middle, first

    def own(u):
        last, middle, first = place(u, c, xx, z, y)
        return gath.at[u, c, last, middle, first]

    consts = [
        pltpu.make_async_copy(filt_hbm, filt, csem.at[0]),
        pltpu.make_async_copy(tab_hbm, tab, csem.at[1]),
        pltpu.make_async_copy(inv_hbm, inv, csem.at[2]),
    ]
    units = [
        pltpu.make_async_copy(pan_hbm.at[u // 2, pl.ds(8 * (u % 2), 8)], own(u), psem.at[u])
        for u in range(4)
    ]
    runs = [pltpu.make_async_copy(x_hbm.at[pl.ds(GROUP * i, GROUP)], x.at[pl.ds(GROUP * i, GROUP)], xsem.at[i])
            for i in range(4)]
    for copy in consts[:2] + units + runs + consts[2:]:
        copy.start()
    lax.fori_loop(1, DEVS, greet, 0)

    def gather_start(phase):
        for u in range(4):
            last, middle, first = place(u, c, xx, z, y)
            axis = ((c * 4 + u) % 3 + min(phase, 2)) % 3
            stride = jnp.where(axis == 0, 2, jnp.where(axis == 1, 8, 32))
            at = jnp.where(axis == 0, xx, jnp.where(axis == 1, z, y))
            if phase < 2:
                block = [gath.at[u, c, last, middle, first], gath.at[u, c, last, middle]][phase]
                sends = [(1, block), (3, block), (2, block)]
            elif phase == 2:
                sends = [(1, gath.at[u, c, last]), (3, gath.at[u, c, last])]
            else:
                sends = [
                    (1, gath.at[u, c, (last + 3) % 4, pl.ds(0, 2)]),
                    (3, gath.at[u, c, (last + 1) % 4, pl.ds(2, 2)]),
                ]
            for step, block in sends:
                to = me + ((at + step) % 4 - at) * stride
                pltpu.make_async_remote_copy(
                    block, block, g_send.at[u, phase], g_recv.at[u, phase],
                    device_id=(to,), device_id_type=MESH,
                ).start()

    def gather_wait(phase):
        for u in range(4):
            three = pl.ds(0, 3)
            block = [
                gath.at[u, c, 0, 0, three],
                gath.at[u, c, 0, three],
                gath.at[u, c, pl.ds(0, 2)],
                gath.at[u, c, 0],
            ][phase]
            whole = pltpu.make_async_remote_copy(
                block, block, g_send.at[u, phase], g_recv.at[u, phase],
                device_id=(partner,), device_id_type=MESH,
            )
            whole.wait_send()
            whole.wait_recv()

    def whiten(i):
        runs[i].wait()
        v, vt = (tab[0], tab[1]), (tab[2], tab[3])
        rows = x[GROUP * i : GROUP * (i + 1)].reshape(GROUP * N, N)
        cols = dot3(split(rows), v)
        backs = []
        for g in range(GROUP):
            t = dot3(vt, split(cols[g * N : (g + 1) * N]))
            low, up = t[:HALF], t[HALF:]
            turned = jnp.concatenate(
                [
                    jnp.concatenate([up[:, HALF:], up[:, :HALF]], axis=1),
                    jnp.concatenate([low[:, HALF:], low[:, :HALF]], axis=1),
                ],
                axis=0,
            )
            backs.append(even[...] * t + odd[...] * turned)
        spread = dot3(split(jnp.concatenate(backs, axis=0)), vt)
        for g in range(GROUP):
            done = dot3(v, split(spread[g * N : (g + 1) * N]))
            for h in range(2):
                out[i, h, pl.ds(g, N, stride=GROUP), :] = done[:, h * HALF : (h + 1) * HALF]

    def send_part(part, low=1, high=DEVS):
        def send(k, carry):
            dx = k % 4
            dy = (dx + (k // 4) % 4) % 4
            dz = (dx + (k // 16) % 4) % 4
            d = ((((y + dy) % 4) * 4 + (z + dz) % 4) * 4 + (xx + dx) % 4) * 2 + (c + k // 64) % 2
            pltpu.make_async_remote_copy(
                out.at[part, :, pl.ds(pl.multiple_of(d * 8, 8), 8)], land.at[:, part, me],
                a_send.at[part], a_recv.at[part], device_id=(d,), device_id_type=MESH,
            ).start()
            return carry

        lax.fori_loop(low, high, send, 0)

    def keep_part(part):
        return pltpu.make_async_copy(
            out.at[part, :, pl.ds(pl.multiple_of(me * 8, 8), 8)], land.at[:, part, me], lsem.at[part]
        )

    def arrived(part):
        keep_part(part).wait()
        rest = pl.ds(0, (DEVS - 1) * 8)
        whole = pltpu.make_async_remote_copy(
            out.at[part, :, rest], out.at[part, :, rest], a_send.at[part], a_recv.at[part],
            device_id=(partner,), device_id_type=MESH,
        )
        whole.wait_send()
        whole.wait_recv()

    consts[0].wait()
    consts[1].wait()
    e, o = coefficients(filt[...])
    even[...] = e
    odd[...] = o
    whiten(0)
    for copy in units:
        copy.wait()
    pl.semaphore_wait(bar, DEVS - 1)
    gather_start(0)
    send_part(0, 1, 12)
    whiten(1)
    gather_wait(0)
    gather_start(1)
    send_part(0, 12)
    whiten(2)
    gather_wait(1)
    gather_start(2)
    send_part(1, 1, 24)
    whiten(3)
    gather_wait(2)
    gather_start(3)
    send_part(1, 24)
    send_part(2)
    send_part(3)
    for part in range(4):
        keep_part(part).start()
    gather_wait(3)

    swaps = []
    for u in range(4):
        block = gath.at[u, c]
        swap = pltpu.make_async_remote_copy(
            block, block, g_send.at[u, 4], g_recv.at[u, 4], device_id=(partner,), device_id_type=MESH
        )
        swap.start()
        swaps.append(swap)
    for swap in swaps:
        swap.wait_send()
        swap.wait_recv()
    consts[2].wait()

    def order(d, carry):
        cy, cz, cx, core = d // 32, (d // 8) % 4, (d // 2) % 4, d % 2
        for u in range(4):
            last, middle, first = place(u, core, cx, cz, cy)
            to = pl.ds(pl.multiple_of(d * 16 + 8 * (u % 2), 8), 8)
            pan[u // 2, to, :] = gath[u, core, last, middle, first]
        return carry

    lax.fori_loop(0, DEVS, order, 0)

    b0, b1 = split(inv[0]), split(inv[1])
    joined = dot3(split(pan[0, N : 2 * N, :]), b0)
    joined_parts = split(joined)
    cross = dot3(b1, joined_parts)

    row = lax.broadcasted_iota(jnp.int32, (N, N), 0)
    col = lax.broadcasted_iota(jnp.int32, (N, N), 1)
    shuffle = (col == (row // 8 % 2) * HALF + row // 16 * 8 + row % 8).astype(BF16)

    def put(start, left, right):
        rows = pl.ds(start, N)
        for side, value in enumerate((left, right)):
            for level, part in enumerate(split(value)):
                moved = dot(part, shuffle).astype(BF16)
                for half in range(2):
                    factor[half, level, rows, HALF * side : HALF * (side + 1)] = moved[
                        :, HALF * half : HALF * (half + 1)
                    ]

    put(0, inv[0], jnp.zeros((N, N), F32))
    put(N, -cross, inv[1])

    def combine(i, carry):
        start = pl.multiple_of(i * N, N)
        h1 = dot3(split(pan[1, pl.ds(start, N), :]), b1)
        h0 = dot3(split(pan[0, pl.ds(start, N), :]), b0) - dot3(split(h1), joined_parts)
        put(start, -h0, -h1)
        return carry

    lax.fori_loop(2, 8, combine, 0)

    def rows_of(half, start, sources):
        lower = lax.broadcasted_iota(jnp.int32, (sources, 8, HALF), 1) < GROUP
        columns = [None] * 4
        for h in range(2):
            a = land[h, 2 * half, pl.ds(start, sources)]
            b = land[h, 2 * half + 1, pl.ds(start, sources)]
            columns[h] = jnp.where(lower, a, pltpu.roll(b, GROUP, 1))
            columns[2 + h] = jnp.where(lower, pltpu.roll(a, GROUP, 1), b)
        return jnp.concatenate(columns, axis=2)

    def multiply(half):
        high, low = split(rows_of(half, 0, 32).reshape(N, 512))
        wh[...] = high
        wl[...] = low

        def chunk(i, own):
            rows = pl.ds(pl.multiple_of(i * N, N), N)
            product = dot3((factor[half, 0, rows, :], factor[half, 1, rows, :]), (wh[...], wl[...]))
            if own:
                mine = rows_of(half, i * 16, 16)
                none = jnp.zeros_like(mine)
                both = [mine, none] if half == 0 else [none, mine]
                product = product + jnp.stack(both, axis=1).reshape(N, 512)
            if half == 0:
                acc[rows, :] = product
            else:
                acc[rows, :] = acc[rows, :] + product

        for i in range(2):
            chunk(i, False)

        def later(i, carry):
            chunk(i, True)
            return carry

        lax.fori_loop(2, 8, later, 0)

    arrived(0)
    arrived(1)
    multiply(0)
    arrived(2)
    arrived(3)
    multiply(1)


def front(runs_field, filter_t, block_inverses, factor_panels, table):
    anywhere = pl.BlockSpec(memory_space=pl.ANY)
    return pl.pallas_call(
        front_kernel,
        out_shape=pltpu.VMEM((2048, 512), F32),
        in_specs=[anywhere] * 5,
        out_specs=pl.BlockSpec(memory_space=pltpu.VMEM),
        scratch_shapes=[
            pltpu.VMEM((16, N, N), F32),
            pltpu.VMEM((129, N), F32),
            pltpu.VMEM((2, N, N), F32),
            pltpu.VMEM((4, N, N), BF16),
            pltpu.VMEM((N, N), F32),
            pltpu.VMEM((N, N), F32),
            pltpu.VMEM((4, 2, 1024, HALF), F32),
            pltpu.VMEM((2, 4, DEVS, 8, HALF), F32),
            pltpu.VMEM((4, 2, 4, 4, 4, 8, N), F32),
            pltpu.VMEM((2, 2048, N), F32),
            pltpu.VMEM((2, 2, 2048, N), BF16),
            pltpu.VMEM((N, 512), BF16),
            pltpu.VMEM((N, 512), BF16),
            pltpu.SemaphoreType.DMA((4,)),
            pltpu.SemaphoreType.DMA((3,)),
            pltpu.SemaphoreType.DMA((4,)),
            pltpu.SemaphoreType.DMA((4,)),
            pltpu.SemaphoreType.DMA((4,)),
            pltpu.SemaphoreType.DMA((4, 5)),
            pltpu.SemaphoreType.DMA((4, 5)),
            pltpu.SemaphoreType.DMA((4,)),
        ],
        compiler_params=pltpu.CompilerParams(
            collective_id=0, has_side_effects=True, vmem_limit_bytes=58 << 20
        ),
        name="front",
    )(runs_field, filter_t, block_inverses, factor_panels, table)


def per_device(runs_field, spectral_filter, block_inverses, factor_panels):
    return front(runs_field, spectral_filter.T, block_inverses, factor_panels, jnp.asarray(tables()))


def solution(mesh):
    return jax.shard_map(
        per_device,
        mesh=mesh,
        in_specs=(P("dev", None, None), P(), P(), P(None, "dev", None)),
        out_specs=P(None, "dev"),
        check_vma=False,
    )
```

```python
import functools
import math

import jax
import jax.numpy as jnp
import numpy as np
from jax import lax
from jax.experimental import pallas as pl
from jax.experimental.pallas import tpu as pltpu
from jax.sharding import PartitionSpec as P

MESH = pl.DeviceIdType.MESH
F32, BF16 = jnp.float32, jnp.bfloat16
N, HALF = 256, 128
DEVS = 128
GROUP = 4


def tables():
    n = np.arange(N)[:, None]
    k = np.arange(HALF)[None, :]
    angle = 2.0 * math.pi * ((n * k) % N) / N
    low = np.sin(angle)
    low[:, 0] = np.where(np.arange(N) % 2 == 0, 1.0, -1.0)
    v = np.concatenate([np.cos(angle), low], axis=1).astype(np.float32)
    high = v.astype(jnp.bfloat16)
    rest = (v - high.astype(np.float32)).astype(jnp.bfloat16)
    return np.stack([high, rest, high.T, rest.T])


def split(value):
    high = value.astype(BF16)
    return high, (value - high.astype(F32)).astype(BF16)


def dot(a, b):
    return jnp.dot(a, b, preferred_element_type=F32)


def dot3(a, b):
    return dot(a[0], b[0]) + (dot(a[0], b[1]) + dot(a[1], b[0]))


def coefficients(filter_t):
    row = lax.broadcasted_iota(jnp.int32, (HALF, N), 0)
    col = lax.broadcasted_iota(jnp.int32, (HALF, N), 1)
    same = (row == col).astype(F32)
    other = ((row + col == N) & (row > 0)).astype(F32)
    nyquist = ((row == 0) & (col == HALF)).astype(F32)
    not_zero = (row > 0).astype(F32)
    picks = [same + other, (same + other) * not_zero + nyquist, (same - other) * not_zero]
    pick = jnp.concatenate(picks, axis=0).astype(BF16)
    one = filter_t.astype(BF16)
    left = filter_t - one.astype(F32)
    two = left.astype(BF16)
    three = (left - two.astype(F32)).astype(BF16)

    def take(part):
        return lax.dot_general(pick, part, (((1,), (1,)), ((), ())), preferred_element_type=F32)

    mixed = (take(three) + take(two)) + take(one)
    lane = lax.broadcasted_iota(jnp.int32, (3 * HALF, HALF), 1)
    scale = jnp.where(lane == 0, 1.0, 2.0).astype(F32) / float(N * N)
    p = mixed[:, :HALF]
    q = jnp.where(lane == 0, mixed[:, HALF : HALF + 1], p)
    p, q = p * scale, q * scale
    even = jnp.concatenate([p[: 2 * HALF], q[: 2 * HALF]], axis=1)
    odd_p, odd_q = p[2 * HALF :], q[2 * HALF :]
    odd = jnp.concatenate(
        [jnp.concatenate([-odd_q, odd_p], axis=1), jnp.concatenate([odd_q, -odd_p], axis=1)], axis=0
    )
    return even, odd


def front_kernel(
    x_hbm, filt_hbm, inv_hbm, pan_hbm, tab_hbm, acc,
    x, filt, inv, tab, even, odd, out, land, gath, pan, factor, wh, wl,
    xsem, csem, psem, a_send, a_recv, g_send, g_recv, lsem,
):
    me = lax.axis_index("dev")
    y, z, xx, c = me // 32, (me // 8) % 4, (me // 2) % 4, me % 2
    partner = me + 1 - 2 * c
    bar = pltpu.get_barrier_semaphore()

    def greet(k, carry):
        pl.semaphore_signal(bar, inc=1, device_id=(lax.rem(me + k, DEVS),), device_id_type=MESH)
        return carry

    def place(u, core, cx, cz, cy):
        rot = (core * 4 + u) % 3
        first = jnp.where(rot == 0, cx, jnp.where(rot == 1, cz, cy))
        middle = jnp.where(rot == 0, cz, jnp.where(rot == 1, cy, cx))
        last = jnp.where(rot == 0, cy, jnp.where(rot == 1, cx, cz))
        return last, middle, first

    def own(u):
        last, middle, first = place(u, c, xx, z, y)
        return gath.at[u, c, last, middle, first]

    consts = [
        pltpu.make_async_copy(filt_hbm, filt, csem.at[0]),
        pltpu.make_async_copy(tab_hbm, tab, csem.at[1]),
        pltpu.make_async_copy(inv_hbm, inv, csem.at[2]),
    ]
    units = [
        pltpu.make_async_copy(pan_hbm.at[u // 2, pl.ds(8 * (u % 2), 8)], own(u), psem.at[u])
        for u in range(4)
    ]
    runs = [pltpu.make_async_copy(x_hbm.at[pl.ds(GROUP * i, GROUP)], x.at[pl.ds(GROUP * i, GROUP)], xsem.at[i])
            for i in range(4)]
    for copy in consts[:2] + units + runs + consts[2:]:
        copy.start()
    lax.fori_loop(1, DEVS, greet, 0)

    def gather_start(phase):
        for u in range(4):
            last, middle, first = place(u, c, xx, z, y)
            axis = ((c * 4 + u) % 3 + min(phase, 2)) % 3
            stride = jnp.where(axis == 0, 2, jnp.where(axis == 1, 8, 32))
            at = jnp.where(axis == 0, xx, jnp.where(axis == 1, z, y))
            if phase < 2:
                block = [gath.at[u, c, last, middle, first], gath.at[u, c, last, middle]][phase]
                sends = [(1, block), (3, block), (2, block)]
            elif phase == 2:
                sends = [(1, gath.at[u, c, last]), (3, gath.at[u, c, last])]
            else:
                sends = [
                    (1, gath.at[u, c, (last + 3) % 4, pl.ds(0, 2)]),
                    (3, gath.at[u, c, (last + 1) % 4, pl.ds(2, 2)]),
                ]
            for step, block in sends:
                to = me + ((at + step) % 4 - at) * stride
                pltpu.make_async_remote_copy(
                    block, block, g_send.at[u, phase], g_recv.at[u, phase],
                    device_id=(to,), device_id_type=MESH,
                ).start()

    def gather_wait(phase):
        for u in range(4):
            three = pl.ds(0, 3)
            block = [
                gath.at[u, c, 0, 0, three],
                gath.at[u, c, 0, three],
                gath.at[u, c, pl.ds(0, 2)],
                gath.at[u, c, 0],
            ][phase]
            whole = pltpu.make_async_remote_copy(
                block, block, g_send.at[u, phase], g_recv.at[u, phase],
                device_id=(partner,), device_id_type=MESH,
            )
            whole.wait_send()
            whole.wait_recv()

    def whiten(i):
        runs[i].wait()
        v, vt = (tab[0], tab[1]), (tab[2], tab[3])
        rows = x[GROUP * i : GROUP * (i + 1)].reshape(GROUP * N, N)
        cols = dot3(split(rows), v)
        backs = []
        for g in range(GROUP):
            t = dot3(vt, split(cols[g * N : (g + 1) * N]))
            low, up = t[:HALF], t[HALF:]
            turned = jnp.concatenate(
                [
                    jnp.concatenate([up[:, HALF:], up[:, :HALF]], axis=1),
                    jnp.concatenate([low[:, HALF:], low[:, :HALF]], axis=1),
                ],
                axis=0,
            )
            backs.append(even[...] * t + odd[...] * turned)
        spread = dot3(split(jnp.concatenate(backs, axis=0)), vt)
        for g in range(GROUP):
            done = dot3(v, split(spread[g * N : (g + 1) * N]))
            for h in range(2):
                out[i, h, pl.ds(g, N, stride=GROUP), :] = done[:, h * HALF : (h + 1) * HALF]

    def send_part(part, low=1, high=DEVS):
        def send(k, carry):
            dx = k % 4
            dy = (dx + (k // 4) % 4) % 4
            dz = (dx + (k // 16) % 4) % 4
            d = ((((y + dy) % 4) * 4 + (z + dz) % 4) * 4 + (xx + dx) % 4) * 2 + (c + k // 64) % 2
            pltpu.make_async_remote_copy(
                out.at[part, :, pl.ds(pl.multiple_of(d * 8, 8), 8)], land.at[:, part, me],
                a_send.at[part], a_recv.at[part], device_id=(d,), device_id_type=MESH,
            ).start()
            return carry

        lax.fori_loop(low, high, send, 0)

    def keep_part(part):
        return pltpu.make_async_copy(
            out.at[part, :, pl.ds(pl.multiple_of(me * 8, 8), 8)], land.at[:, part, me], lsem.at[part]
        )

    def arrived(part):
        keep_part(part).wait()
        rest = pl.ds(0, (DEVS - 1) * 8)
        whole = pltpu.make_async_remote_copy(
            out.at[part, :, rest], out.at[part, :, rest], a_send.at[part], a_recv.at[part],
            device_id=(partner,), device_id_type=MESH,
        )
        whole.wait_send()
        whole.wait_recv()

    consts[0].wait()
    consts[1].wait()
    e, o = coefficients(filt[...])
    even[...] = e
    odd[...] = o
    whiten(0)
    for copy in units:
        copy.wait()
    pl.semaphore_wait(bar, DEVS - 1)
    gather_start(0)
    send_part(0, 1, 12)
    whiten(1)
    gather_wait(0)
    gather_start(1)
    send_part(0, 12)
    whiten(2)
    gather_wait(1)
    gather_start(2)
    send_part(1, 1, 36)
    whiten(3)
    gather_wait(2)
    gather_start(3)
    send_part(1, 36)
    send_part(2)
    send_part(3)
    for part in range(4):
        keep_part(part).start()
    gather_wait(3)

    swaps = []
    for u in range(4):
        block = gath.at[u, c]
        swap = pltpu.make_async_remote_copy(
            block, block, g_send.at[u, 4], g_recv.at[u, 4], device_id=(partner,), device_id_type=MESH
        )
        swap.start()
        swaps.append(swap)

    def order(e, carry, core):
        cy, cz, cx = e // 16, (e // 4) % 4, e % 4
        d = e * 2 + core
        for u in range(4):
            last, middle, first = place(u, core, cx, cz, cy)
            to = pl.ds(pl.multiple_of(d * 16 + 8 * (u % 2), 8), 8)
            pan[u // 2, to, :] = gath[u, core, last, middle, first]
        return carry

    lax.fori_loop(0, DEVS // 2, functools.partial(order, core=c), 0)
    for swap in swaps:
        swap.wait_send()
        swap.wait_recv()
    consts[2].wait()
    lax.fori_loop(0, DEVS // 2, functools.partial(order, core=1 - c), 0)

    b0, b1 = split(inv[0]), split(inv[1])
    joined = dot3(split(pan[0, N : 2 * N, :]), b0)
    joined_parts = split(joined)
    cross = dot3(b1, joined_parts)

    row = lax.broadcasted_iota(jnp.int32, (N, N), 0)
    col = lax.broadcasted_iota(jnp.int32, (N, N), 1)
    shuffle = (col == (row // 8 % 2) * HALF + row // 16 * 8 + row % 8).astype(BF16)

    def put(start, left, right):
        rows = pl.ds(start, N)
        for side, value in enumerate((left, right)):
            for level, part in enumerate(split(value)):
                moved = dot(part, shuffle).astype(BF16)
                for half in range(2):
                    factor[half, level, rows, HALF * side : HALF * (side + 1)] = moved[
                        :, HALF * half : HALF * (half + 1)
                    ]

    put(0, inv[0], jnp.zeros((N, N), F32))
    put(N, -cross, inv[1])

    def combine(i, carry):
        start = pl.multiple_of(i * N, N)
        h1 = dot3(split(pan[1, pl.ds(start, N), :]), b1)
        h0 = dot3(split(pan[0, pl.ds(start, N), :]), b0) - dot3(split(h1), joined_parts)
        put(start, -h0, -h1)
        return carry

    lax.fori_loop(2, 8, combine, 0)

    def rows_of(half, start, sources):
        lower = lax.broadcasted_iota(jnp.int32, (sources, 8, HALF), 1) < GROUP
        columns = [None] * 4
        for h in range(2):
            a = land[h, 2 * half, pl.ds(start, sources)]
            b = land[h, 2 * half + 1, pl.ds(start, sources)]
            columns[h] = jnp.where(lower, a, pltpu.roll(b, GROUP, 1))
            columns[2 + h] = jnp.where(lower, pltpu.roll(a, GROUP, 1), b)
        return jnp.concatenate(columns, axis=2)

    def multiply(half):
        high, low = split(rows_of(half, 0, 32).reshape(N, 512))
        wh[...] = high
        wl[...] = low

        def chunk(i, own):
            rows = pl.ds(i * 512, 512)
            high, low = factor[half, 0, rows, :], factor[half, 1, rows, :]
            product = dot(jnp.concatenate([high, low, high], axis=1), jnp.concatenate([wh[...], wh[...], wl[...]], axis=0))
            if own:
                mine = rows_of(half, i * 32, 32)
                none = jnp.zeros_like(mine)
                both = [mine, none] if half == 0 else [none, mine]
                product = product + jnp.stack(both, axis=1).reshape(512, 512)
            if half == 0:
                acc[rows, :] = product
            else:
                acc[rows, :] = acc[rows, :] + product

        chunk(0, False)

        def later(i, carry):
            chunk(i, True)
            return carry

        for i in range(1, 4):
            later(i, 0)

    arrived(0)
    arrived(1)
    multiply(0)
    arrived(2)
    arrived(3)
    multiply(1)


def front(runs_field, filter_t, block_inverses, factor_panels, table):
    anywhere = pl.BlockSpec(memory_space=pl.ANY)
    return pl.pallas_call(
        front_kernel,
        out_shape=pltpu.VMEM((2048, 512), F32),
        in_specs=[anywhere] * 5,
        out_specs=pl.BlockSpec(memory_space=pltpu.VMEM),
        scratch_shapes=[
            pltpu.VMEM((16, N, N), F32),
            pltpu.VMEM((129, N), F32),
            pltpu.VMEM((2, N, N), F32),
            pltpu.VMEM((4, N, N), BF16),
            pltpu.VMEM((N, N), F32),
            pltpu.VMEM((N, N), F32),
            pltpu.VMEM((4, 2, 1024, HALF), F32),
            pltpu.VMEM((2, 4, DEVS, 8, HALF), F32),
            pltpu.VMEM((4, 2, 4, 4, 4, 8, N), F32),
            pltpu.VMEM((2, 2048, N), F32),
            pltpu.VMEM((2, 2, 2048, N), BF16),
            pltpu.VMEM((N, 512), BF16),
            pltpu.VMEM((N, 512), BF16),
            pltpu.SemaphoreType.DMA((4,)),
            pltpu.SemaphoreType.DMA((3,)),
            pltpu.SemaphoreType.DMA((4,)),
            pltpu.SemaphoreType.DMA((4,)),
            pltpu.SemaphoreType.DMA((4,)),
            pltpu.SemaphoreType.DMA((4, 5)),
            pltpu.SemaphoreType.DMA((4, 5)),
            pltpu.SemaphoreType.DMA((4,)),
        ],
        compiler_params=pltpu.CompilerParams(
            collective_id=0, has_side_effects=True, vmem_limit_bytes=58 << 20
        ),
        name="front",
    )(runs_field, filter_t, block_inverses, factor_panels, table)


def per_device(runs_field, spectral_filter, block_inverses, factor_panels):
    return front(runs_field, spectral_filter.T, block_inverses, factor_panels, jnp.asarray(tables()))


def solution(mesh):
    return jax.shard_map(
        per_device,
        mesh=mesh,
        in_specs=(P("dev", None, None), P(), P(), P(None, "dev", None)),
        out_specs=P(None, "dev"),
        check_vma=False,
    )
```

```python
import functools
import math

import jax
import jax.numpy as jnp
import numpy as np
from jax import lax
from jax.experimental import pallas as pl
from jax.experimental.pallas import tpu as pltpu
from jax.sharding import PartitionSpec as P

MESH = pl.DeviceIdType.MESH
F32, BF16 = jnp.float32, jnp.bfloat16
N, HALF = 256, 128
DEVS = 128
GROUP = 4


def tables():
    n = np.arange(N)[:, None]
    k = np.arange(HALF)[None, :]
    angle = 2.0 * math.pi * ((n * k) % N) / N
    low = np.sin(angle)
    low[:, 0] = np.where(np.arange(N) % 2 == 0, 1.0, -1.0)
    v = np.concatenate([np.cos(angle), low], axis=1).astype(np.float32)
    high = v.astype(jnp.bfloat16)
    rest = (v - high.astype(np.float32)).astype(jnp.bfloat16)
    return np.stack([high, rest, high.T, rest.T])


def split(value):
    high = value.astype(BF16)
    return high, (value - high.astype(F32)).astype(BF16)


def dot(a, b):
    return jnp.dot(a, b, preferred_element_type=F32)


def dot3(a, b):
    return dot(a[0], b[0]) + (dot(a[0], b[1]) + dot(a[1], b[0]))


def coefficients(filter_t):
    row = lax.broadcasted_iota(jnp.int32, (HALF, N), 0)
    col = lax.broadcasted_iota(jnp.int32, (HALF, N), 1)
    same = (row == col).astype(F32)
    other = ((row + col == N) & (row > 0)).astype(F32)
    nyquist = ((row == 0) & (col == HALF)).astype(F32)
    not_zero = (row > 0).astype(F32)
    picks = [same + other, (same + other) * not_zero + nyquist, (same - other) * not_zero]
    pick = jnp.concatenate(picks, axis=0).astype(BF16)
    one = filter_t.astype(BF16)
    left = filter_t - one.astype(F32)
    two = left.astype(BF16)
    three = (left - two.astype(F32)).astype(BF16)

    def take(part):
        return lax.dot_general(pick, part, (((1,), (1,)), ((), ())), preferred_element_type=F32)

    mixed = (take(three) + take(two)) + take(one)
    lane = lax.broadcasted_iota(jnp.int32, (3 * HALF, HALF), 1)
    scale = jnp.where(lane == 0, 1.0, 2.0).astype(F32) / float(N * N)
    p = mixed[:, :HALF]
    q = jnp.where(lane == 0, mixed[:, HALF : HALF + 1], p)
    p, q = p * scale, q * scale
    even = jnp.concatenate([p[: 2 * HALF], q[: 2 * HALF]], axis=1)
    odd_p, odd_q = p[2 * HALF :], q[2 * HALF :]
    odd = jnp.concatenate(
        [jnp.concatenate([-odd_q, odd_p], axis=1), jnp.concatenate([odd_q, -odd_p], axis=1)], axis=0
    )
    return even, odd


def front_kernel(
    x_hbm, filt_hbm, inv_hbm, pan_hbm, tab_hbm, acc,
    x, filt, inv, tab, even, odd, out, land, gath, pan, factor, wh, wl,
    xsem, csem, psem, a_send, a_recv, g_send, g_recv, lsem,
):
    me = lax.axis_index("dev")
    y, z, xx, c = me // 32, (me // 8) % 4, (me // 2) % 4, me % 2
    partner = me + 1 - 2 * c
    bar = pltpu.get_barrier_semaphore()

    def greet(k, carry):
        pl.semaphore_signal(bar, inc=1, device_id=(lax.rem(me + k, DEVS),), device_id_type=MESH)
        return carry

    def place(u, core, cx, cz, cy):
        rot = (core * 4 + u) % 3
        first = jnp.where(rot == 0, cx, jnp.where(rot == 1, cz, cy))
        middle = jnp.where(rot == 0, cz, jnp.where(rot == 1, cy, cx))
        last = jnp.where(rot == 0, cy, jnp.where(rot == 1, cx, cz))
        return last, middle, first

    def own(u):
        last, middle, first = place(u, c, xx, z, y)
        return gath.at[u, c, last, middle, first]

    consts = [
        pltpu.make_async_copy(filt_hbm, filt, csem.at[0]),
        pltpu.make_async_copy(tab_hbm, tab, csem.at[1]),
        pltpu.make_async_copy(inv_hbm, inv, csem.at[2]),
    ]
    units = [
        pltpu.make_async_copy(pan_hbm.at[u // 2, pl.ds(8 * (u % 2), 8)], own(u), psem.at[u])
        for u in range(4)
    ]
    runs = [pltpu.make_async_copy(x_hbm.at[pl.ds(GROUP * i, GROUP)], x.at[pl.ds(GROUP * i, GROUP)], xsem.at[i])
            for i in range(4)]
    for copy in consts[:2] + units + runs + consts[2:]:
        copy.start()
    lax.fori_loop(1, DEVS, greet, 0)

    def gather_start(phase):
        for u in range(4):
            last, middle, first = place(u, c, xx, z, y)
            axis = ((c * 4 + u) % 3 + min(phase, 2)) % 3
            stride = jnp.where(axis == 0, 2, jnp.where(axis == 1, 8, 32))
            at = jnp.where(axis == 0, xx, jnp.where(axis == 1, z, y))
            if phase < 2:
                block = [gath.at[u, c, last, middle, first], gath.at[u, c, last, middle]][phase]
                sends = [(1, block), (3, block), (2, block)]
            elif phase == 2:
                sends = [(1, gath.at[u, c, last]), (3, gath.at[u, c, last])]
            else:
                sends = [
                    (1, gath.at[u, c, (last + 3) % 4, pl.ds(0, 2)]),
                    (3, gath.at[u, c, (last + 1) % 4, pl.ds(2, 2)]),
                ]
            for step, block in sends:
                to = me + ((at + step) % 4 - at) * stride
                pltpu.make_async_remote_copy(
                    block, block, g_send.at[u, phase], g_recv.at[u, phase],
                    device_id=(to,), device_id_type=MESH,
                ).start()

    def gather_wait(phase):
        for u in range(4):
            three = pl.ds(0, 3)
            block = [
                gath.at[u, c, 0, 0, three],
                gath.at[u, c, 0, three],
                gath.at[u, c, pl.ds(0, 2)],
                gath.at[u, c, 0],
            ][phase]
            whole = pltpu.make_async_remote_copy(
                block, block, g_send.at[u, phase], g_recv.at[u, phase],
                device_id=(partner,), device_id_type=MESH,
            )
            whole.wait_send()
            whole.wait_recv()

    def whiten(i):
        runs[i].wait()
        v, vt = (tab[0], tab[1]), (tab[2], tab[3])
        rows = x[GROUP * i : GROUP * (i + 1)].reshape(GROUP * N, N)
        cols = dot3(split(rows), v)
        backs = []
        for g in range(GROUP):
            t = dot3(vt, split(cols[g * N : (g + 1) * N]))
            low, up = t[:HALF], t[HALF:]
            turned = jnp.concatenate(
                [
                    jnp.concatenate([up[:, HALF:], up[:, :HALF]], axis=1),
                    jnp.concatenate([low[:, HALF:], low[:, :HALF]], axis=1),
                ],
                axis=0,
            )
            backs.append(even[...] * t + odd[...] * turned)
        spread = dot3(split(jnp.concatenate(backs, axis=0)), vt)
        for g in range(GROUP):
            done = dot3(v, split(spread[g * N : (g + 1) * N]))
            for h in range(2):
                out[i, h, pl.ds(g, N, stride=GROUP), :] = done[:, h * HALF : (h + 1) * HALF]

    def send_part(part, low=1, high=DEVS):
        def send(k, carry):
            dx = k % 4
            dy = (dx + (k // 4) % 4) % 4
            dz = (dx + (k // 16) % 4) % 4
            d = ((((y + dy) % 4) * 4 + (z + dz) % 4) * 4 + (xx + dx) % 4) * 2 + (c + k // 64) % 2
            pltpu.make_async_remote_copy(
                out.at[part, :, pl.ds(pl.multiple_of(d * 8, 8), 8)], land.at[:, part, me],
                a_send.at[part], a_recv.at[part], device_id=(d,), device_id_type=MESH,
            ).start()
            return carry

        lax.fori_loop(low, high, send, 0)

    def keep_part(part):
        return pltpu.make_async_copy(
            out.at[part, :, pl.ds(pl.multiple_of(me * 8, 8), 8)], land.at[:, part, me], lsem.at[part]
        )

    def arrived(part):
        keep_part(part).wait()
        rest = pl.ds(0, (DEVS - 1) * 8)
        whole = pltpu.make_async_remote_copy(
            out.at[part, :, rest], out.at[part, :, rest], a_send.at[part], a_recv.at[part],
            device_id=(partner,), device_id_type=MESH,
        )
        whole.wait_send()
        whole.wait_recv()

    consts[0].wait()
    consts[1].wait()
    e, o = coefficients(filt[...])
    even[...] = e
    odd[...] = o
    whiten(0)
    for copy in units:
        copy.wait()
    pl.semaphore_wait(bar, DEVS - 1)
    gather_start(0)
    send_part(0, 1, 12)
    whiten(1)
    gather_wait(0)
    gather_start(1)
    send_part(0, 12)
    whiten(2)
    gather_wait(1)
    gather_start(2)
    send_part(1, 1, 36)
    whiten(3)
    gather_wait(2)
    gather_start(3)
    send_part(1, 36)
    send_part(2)
    send_part(3)
    for part in range(4):
        keep_part(part).start()
    gather_wait(3)

    swaps = []
    for u in range(4):
        block = gath.at[u, c]
        swap = pltpu.make_async_remote_copy(
            block, block, g_send.at[u, 4], g_recv.at[u, 4], device_id=(partner,), device_id_type=MESH
        )
        swap.start()
        swaps.append(swap)

    def order(e, carry, core):
        cy, cz, cx = e // 16, (e // 4) % 4, e % 4
        d = e * 2 + core
        for u in range(4):
            last, middle, first = place(u, core, cx, cz, cy)
            to = pl.ds(pl.multiple_of(d * 16 + 8 * (u % 2), 8), 8)
            pan[u // 2, to, :] = gath[u, core, last, middle, first]
        return carry

    lax.fori_loop(0, DEVS // 2, functools.partial(order, core=c), 0)
    for swap in swaps:
        swap.wait_send()
        swap.wait_recv()
    consts[2].wait()
    lax.fori_loop(0, DEVS // 2, functools.partial(order, core=1 - c), 0)

    b0, b1 = split(inv[0]), split(inv[1])
    joined = dot3(split(pan[0, N : 2 * N, :]), b0)
    joined_parts = split(joined)
    cross = dot3(b1, joined_parts)

    row = lax.broadcasted_iota(jnp.int32, (N, N), 0)
    col = lax.broadcasted_iota(jnp.int32, (N, N), 1)
    shuffle = (col == (row // 8 % 2) * HALF + row // 16 * 8 + row % 8).astype(BF16)

    def put(start, left, right):
        rows = pl.ds(start, left.shape[0])
        for side, value in enumerate((left, right)):
            for level, part in enumerate(split(value)):
                moved = dot(part, shuffle).astype(BF16)
                for half in range(2):
                    factor[half, level, rows, HALF * side : HALF * (side + 1)] = moved[
                        :, HALF * half : HALF * (half + 1)
                    ]

    put(0, inv[0], jnp.zeros((N, N), F32))
    put(N, -cross, inv[1])

    def combine(i, carry):
        start = i * 512
        h1 = dot3(split(pan[1, pl.ds(start, 512), :]), b1)
        h0 = dot3(split(pan[0, pl.ds(start, 512), :]), b0) - dot3(split(h1), joined_parts)
        put(start, -h0, -h1)
        return carry

    for i in range(1, 4):
        combine(i, 0)

    def rows_of(half, start, sources):
        lower = lax.broadcasted_iota(jnp.int32, (sources, 8, HALF), 1) < GROUP
        columns = [None] * 4
        for h in range(2):
            a = land[h, 2 * half, pl.ds(start, sources)]
            b = land[h, 2 * half + 1, pl.ds(start, sources)]
            columns[h] = jnp.where(lower, a, pltpu.roll(b, GROUP, 1))
            columns[2 + h] = jnp.where(lower, pltpu.roll(a, GROUP, 1), b)
        return jnp.concatenate(columns, axis=2)

    def multiply(half):
        high, low = split(rows_of(half, 0, 32).reshape(N, 512))
        wh[...] = high
        wl[...] = low

        def chunk(i, own):
            rows = pl.ds(i * 512, 512)
            high, low = factor[half, 0, rows, :], factor[half, 1, rows, :]
            product = dot(jnp.concatenate([high, low, high], axis=1), jnp.concatenate([wh[...], wh[...], wl[...]], axis=0))
            if own:
                mine = rows_of(half, i * 32, 32)
                none = jnp.zeros_like(mine)
                both = [mine, none] if half == 0 else [none, mine]
                product = product + jnp.stack(both, axis=1).reshape(512, 512)
            if half == 0:
                acc[rows, :] = product
            else:
                acc[rows, :] = acc[rows, :] + product

        chunk(0, False)

        def later(i, carry):
            chunk(i, True)
            return carry

        for i in range(1, 4):
            later(i, 0)

    arrived(0)
    arrived(1)
    multiply(0)
    arrived(2)
    arrived(3)
    multiply(1)


def front(runs_field, filter_t, block_inverses, factor_panels, table):
    anywhere = pl.BlockSpec(memory_space=pl.ANY)
    return pl.pallas_call(
        front_kernel,
        out_shape=pltpu.VMEM((2048, 512), F32),
        in_specs=[anywhere] * 5,
        out_specs=pl.BlockSpec(memory_space=pltpu.VMEM),
        scratch_shapes=[
            pltpu.VMEM((16, N, N), F32),
            pltpu.VMEM((129, N), F32),
            pltpu.VMEM((2, N, N), F32),
            pltpu.VMEM((4, N, N), BF16),
            pltpu.VMEM((N, N), F32),
            pltpu.VMEM((N, N), F32),
            pltpu.VMEM((4, 2, 1024, HALF), F32),
            pltpu.VMEM((2, 4, DEVS, 8, HALF), F32),
            pltpu.VMEM((4, 2, 4, 4, 4, 8, N), F32),
            pltpu.VMEM((2, 2048, N), F32),
            pltpu.VMEM((2, 2, 2048, N), BF16),
            pltpu.VMEM((N, 512), BF16),
            pltpu.VMEM((N, 512), BF16),
            pltpu.SemaphoreType.DMA((4,)),
            pltpu.SemaphoreType.DMA((3,)),
            pltpu.SemaphoreType.DMA((4,)),
            pltpu.SemaphoreType.DMA((4,)),
            pltpu.SemaphoreType.DMA((4,)),
            pltpu.SemaphoreType.DMA((4, 5)),
            pltpu.SemaphoreType.DMA((4, 5)),
            pltpu.SemaphoreType.DMA((4,)),
        ],
        compiler_params=pltpu.CompilerParams(
            collective_id=0, has_side_effects=True, vmem_limit_bytes=58 << 20
        ),
        name="front",
    )(runs_field, filter_t, block_inverses, factor_panels, table)


def per_device(runs_field, spectral_filter, block_inverses, factor_panels):
    return front(runs_field, spectral_filter.T, block_inverses, factor_panels, jnp.asarray(tables()))


def solution(mesh):
    return jax.shard_map(
        per_device,
        mesh=mesh,
        in_specs=(P("dev", None, None), P(), P(), P(None, "dev", None)),
        out_specs=P(None, "dev"),
        check_vma=False,
    )
```
